32 devices in a mesh: dp: 8 (over y, x, core), seq: 4 (over z).
Axes of the slice: x: 2, y: 2, z: 4, core: 2. Of those that a mesh axis runs over, the one named last changes fastest.
Arguments:
- inputs: bfloat16 [32768, 768], P(('dp', 'seq')), may hold values from -6 to 6
- attn_gain: bfloat16 [768], P('dp'), may hold values from 0.25 to 1.75
- qkv_weight: bfloat16 [768, 2304], P('dp'), may hold values from -0.25 to 0.25
- proj_weight: bfloat16 [768, 768], P('dp'), may hold values from -0.4375 to 0.4375
- mlp_gain: bfloat16 [768], P('dp'), may hold values from 0.25 to 1.75
- in_weight: bfloat16 [768, 2304], P('dp'), may hold values from -0.21875 to 0.21875
- out_weight: bfloat16 [1152, 768], P('dp'), may hold values from -0.25 to 0.25
- cotangent: bfloat16 [32768, 768], P(('dp', 'seq')), may hold values from -12 to 12
Outputs:
- output: bfloat16 [32768, 768], P(('dp', 'seq'))
- input_grad: bfloat16 [32768, 768], P(('dp', 'seq'))
- attn_gain_grad: float32 [768], P('dp')
- qkv_weight_grad: float32 [768, 2304], P('dp')
- proj_weight_grad: float32 [768, 768], P('dp')
- mlp_gain_grad: float32 [768], P('dp')
- in_weight_grad: float32 [768, 2304], P('dp')
- out_weight_grad: float32 [1152, 768], P('dp')
The draws below stay inside these ranges and needn't reach their ends.
All inputs are finite; a program needn't handle non-finite values.
Results may differ from the reference program's by a relative error of at most 0.02.
Values may be sent and summed in bfloat16 or wider, within the bound.
A program may use at most 128 MiB of HBM per device.

```python
import jax
import jax.numpy as jnp
from jax import lax

D = 768
HEADS = 12
HEAD_DIM = 64
FF = 1152
WINDOW = 64
QBLOCK = 512
SEQ_LEN = 4096
TOKENS = 32768
N_DP = 8


def with_spikes(array, own_key, source, target, blocks, factor):
    def block_of(dim):
        return (jnp.arange(array.shape[dim]) // (array.shape[dim] // blocks)).reshape((-1,) + (1,) * (array.ndim - 1 - dim))

    near = jax.random.permutation(own_key, blocks)[block_of(target)]
    far = (block_of(target) + blocks // 2) % blocks
    return jnp.where((block_of(source) == near) | (block_of(source) == far), factor * array, array)


def block_scale(rng, extent, pieces, smallest, high):
    level, own = 1.0, jax.random.fold_in(rng, 6)
    for dim, parts in pieces:
        heights = jnp.exp(jax.random.uniform(jax.random.fold_in(own, dim), (parts,), jnp.float32, smallest / len(pieces), high / len(pieces)))
        level = level * jnp.repeat(heights, extent[dim] // parts).reshape([-1 if axis == dim else 1 for axis in range(len(extent))])
    return level


def bell_draw(key, shape, scale, most, pieces=(), kind=jnp.bfloat16):
    values = scale * jax.random.normal(key, shape, jnp.float32)
    if pieces:
        values = values * block_scale(key, shape, pieces, -0.22, 0.18)
    return jnp.clip(values, -most, most).astype(kind)


def gaussian_with(key, shape, scale, bound, pieces, heavy, kind=jnp.bfloat16):
    drawn = scale * jax.random.normal(key, shape, jnp.float32)
    if pieces:
        drawn = drawn * block_scale(key, shape, pieces, -0.22, 0.18)
    return jnp.clip(with_spikes(drawn, jax.random.fold_in(key, 3), *heavy), -bound, bound).astype(kind)


def setup_inputs(seed: int = 0) -> dict:
    seeds = jax.random.split(jax.random.key(seed), 9)
    return {
        "inputs": bell_draw(seeds[0], (TOKENS, D), 1.0, 6.0, ((0, 32),)),
        "attn_gain": jnp.clip(1.0 + 0.15 * jax.random.normal(seeds[1], (D,), jnp.float32), 0.25, 1.75).astype(jnp.bfloat16),
        "qkv_weight": bell_draw(seeds[2], (D, 3 * D), (D * 2 // 3) ** -0.5, 0.25, ((0, 8),)),
        "proj_weight": bell_draw(seeds[3], (D, D), (D // 4) ** -0.5, 0.4375, ((0, 8),)),
        "mlp_gain": jnp.clip(1.0 + 0.15 * jax.random.normal(seeds[4], (D,), jnp.float32), 0.25, 1.75).astype(jnp.bfloat16),
        "in_weight": bell_draw(seeds[5], (D, 2 * FF), D ** -0.5, 0.21875, ((0, 8),)),
        "out_weight": bell_draw(seeds[6], (FF, D), (FF // 2) ** -0.5, 0.25, ((0, 8),)),
        "cotangent": gaussian_with(seeds[7], (TOKENS, D), 1.0, 12.0, ((0, 32),), (0, 1, 32, 2.75)),
    }


@jax.custom_vjp
def low(v):
    return lax.optimization_barrier(v.astype(jnp.bfloat16)).astype(jnp.float32)

@jax.custom_vjp
def low_back(v):
    return v

def low_keep(v):
    return (low(v), None)

def low_pass(kept, grad):
    return (grad,)

def back_keep(v):
    return (v, None)

def back_low(kept, grad):
    return (low(grad),)
low.defvjp(low_keep, low_pass)
low_back.defvjp(back_keep, back_low)
epsilon = 1e-05
theta_base = 10000.0
masked_score = -1e+30

def layer_norm(features, gain_vector):
    center = features - lax.optimization_barrier(jnp.mean(features, -1, keepdims=True))
    spread = lax.optimization_barrier(jnp.mean(center * center, -1, keepdims=True))
    return center * lax.rsqrt(spread + epsilon) * gain_vector

def rotary_tables(positions, head_width):
    half_width = head_width // 2
    inverse_freq = theta_base ** (-(jnp.arange(half_width, dtype=jnp.float32) * 2.0) / head_width)
    angles = positions[:, None] * inverse_freq[None, :]
    cosine_table = jnp.concatenate([jnp.cos(angles), jnp.cos(angles)], -1)
    sine_table = jnp.concatenate([jnp.sin(angles), jnp.sin(angles)], -1)
    return (cosine_table[:, None, :], sine_table[:, None, :])

def rotate(features, cosine_table, sine_table):
    half_width = features.shape[-1] // 2
    turned = jnp.concatenate([-features[..., half_width:], features[..., :half_width]], -1)
    return features * cosine_table + turned * sine_table

def gated_gelu(up_values):
    gelu_input = up_values[:, :FF]
    gate_half = up_values[:, FF:]
    return jax.nn.gelu(gelu_input, approximate=False) * gate_half

def band_attention(queries, key_all, value_all):
    row_count = queries.shape[0]
    key_span = QBLOCK + 2 * WINDOW
    score_scale = HEAD_DIM ** (-0.5)
    highest = lax.Precision.HIGHEST
    key_pad = jnp.pad(key_all, ((WINDOW, WINDOW), (0, 0), (0, 0)))
    value_pad = jnp.pad(value_all, ((WINDOW, WINDOW), (0, 0), (0, 0)))

    def one_block(block_index):
        row_start = block_index * QBLOCK
        query_block = lax.dynamic_slice_in_dim(queries, row_start, QBLOCK, 0)
        key_block = lax.dynamic_slice_in_dim(key_pad, row_start, key_span, 0)
        value_block = lax.dynamic_slice_in_dim(value_pad, row_start, key_span, 0)
        scores = low_back(jnp.einsum('qhd,khd->hqk', query_block, key_block, precision=highest) * score_scale)
        query_pos = row_start + jnp.arange(QBLOCK, dtype=jnp.int32)[:, None]
        key_pos = row_start - WINDOW + jnp.arange(key_span, dtype=jnp.int32)[None, :]
        in_band = (jnp.abs(query_pos - key_pos) <= WINDOW) & (key_pos >= 0) & (key_pos < row_count)
        scores = jnp.where(in_band[None], scores, masked_score)
        row_max = lax.optimization_barrier(jnp.max(scores, -1, keepdims=True))
        weights = jnp.exp(scores - row_max)
        softmax_out = weights / lax.optimization_barrier(jnp.sum(weights, -1, keepdims=True))
        return jnp.einsum('hqk,khd->qhd', low(softmax_out), value_block, precision=highest)
    blocks = lax.map(jax.checkpoint(one_block), jnp.arange(row_count // QBLOCK, dtype=jnp.int32))
    return blocks.reshape(queries.shape)

def layer_forward(sequence, attn_gain, qkv_weight, proj_weight, mlp_gain, in_weight, out_weight):
    length = sequence.shape[0]
    highest = lax.Precision.HIGHEST
    normed = low(layer_norm(sequence, attn_gain))
    projected = low_back(jnp.dot(normed, qkv_weight, precision=highest))
    positions = jnp.arange(length, dtype=jnp.int32).astype(jnp.float32)
    cosine_table, sine_table = rotary_tables(positions, HEAD_DIM)
    query_all = rotate(projected[:, :D].reshape(length, HEADS, HEAD_DIM), cosine_table, sine_table)
    key_all = rotate(projected[:, D:2 * D].reshape(length, HEADS, HEAD_DIM), cosine_table, sine_table)
    value_all = projected[:, 2 * D:].reshape(length, HEADS, HEAD_DIM)
    query_all = low_back(low(query_all))
    key_all = low_back(low(key_all))
    value_all = low_back(low(value_all))
    mixed = low_back(low(band_attention(query_all, key_all, value_all).reshape(length, D)))
    hidden_state = sequence + low_back(jnp.dot(mixed, proj_weight, precision=highest))
    normed_two = low(layer_norm(hidden_state, mlp_gain))
    up_values = low_back(jnp.dot(normed_two, in_weight, precision=highest))
    gated = low(gated_gelu(up_values))
    return hidden_state + low_back(jnp.dot(gated, out_weight, precision=highest))

def reference(inputs, attn_gain, qkv_weight, proj_weight, mlp_gain, in_weight, out_weight, cotangent):
    params = (attn_gain.astype(jnp.float32), qkv_weight.astype(jnp.float32), proj_weight.astype(jnp.float32), mlp_gain.astype(jnp.float32), in_weight.astype(jnp.float32), out_weight.astype(jnp.float32))
    sequences = inputs.astype(jnp.float32).reshape(N_DP, SEQ_LEN, D)
    cotangents = cotangent.astype(jnp.float32).reshape(N_DP, SEQ_LEN, D)

    def one_sequence(totals, seq_pair):
        sequence, grad_seq = seq_pair
        result, backward = jax.vjp(layer_forward, sequence, *params)
        gradients = backward(grad_seq)
        totals = (totals[0] + gradients[1], totals[1] + gradients[2], totals[2] + gradients[3], totals[3] + gradients[4], totals[4] + gradients[5], totals[5] + gradients[6])
        return (totals, (result, gradients[0]))
    zero_sums = (jnp.zeros((D,), jnp.float32), jnp.zeros((D, 3 * D), jnp.float32), jnp.zeros((D, D), jnp.float32), jnp.zeros((D,), jnp.float32), jnp.zeros((D, 2 * FF), jnp.float32), jnp.zeros((FF, D), jnp.float32))
    totals, outputs = lax.scan(one_sequence, zero_sums, (sequences, cotangents))
    results, input_grads = outputs
    return (results.reshape(TOKENS, D).astype(jnp.bfloat16), input_grads.reshape(TOKENS, D).astype(jnp.bfloat16), totals[0], totals[1], totals[2], totals[3], totals[4], totals[5])
```

```python
import jax
import jax.numpy as jnp
from jax import lax
from jax.experimental import pallas as pl
from jax.experimental.pallas import tpu as pltpu
from jax.sharding import PartitionSpec as P

D = 768
HEADS = 12
HEAD_DIM = 64
FF = 1152
WINDOW = 64
BLOCK = 128
SPAN = BLOCK + 2 * WINDOW
PAIR = 2 * HEAD_DIM

epsilon = 1e-05
theta_base = 10000.0
masked_score = -1e30
bf16, f32 = jnp.bfloat16, jnp.float32


def norm_parts(features):
    center = features - jnp.mean(features, -1, keepdims=True)
    spread = jnp.mean(center * center, -1, keepdims=True)
    scale = lax.rsqrt(spread + epsilon)
    return center * scale, scale


def norm_back(grad, xhat, scale):
    return scale * (
        grad - jnp.mean(grad, -1, keepdims=True) - xhat * jnp.mean(grad * xhat, -1, keepdims=True)
    )


def rotary_tables(positions):
    half = HEAD_DIM // 2
    inverse_freq = theta_base ** (-(jnp.arange(half, dtype=f32) * 2.0) / HEAD_DIM)
    angles = positions[:, None] * inverse_freq[None, :]
    cosine, sine = jnp.cos(angles), jnp.sin(angles)
    return (
        jnp.concatenate([cosine, cosine, cosine, cosine], -1),
        jnp.concatenate([-sine, sine, -sine, sine], -1),
    )


def turn(values):
    lane = lax.broadcasted_iota(jnp.int32, values.shape, 1)
    low_half = (lane & (HEAD_DIM - 1)) < HEAD_DIM // 2
    return jnp.where(
        low_half,
        pltpu.roll(values, PAIR - HEAD_DIM // 2, 1),
        pltpu.roll(values, HEAD_DIM // 2, 1),
    )


def split_heads(pair):
    lane = lax.broadcasted_iota(jnp.int32, pair.shape, 1)
    zero = jnp.zeros_like(pair)
    first = jnp.where(lane < HEAD_DIM, pair, zero)
    second = jnp.where(lane < HEAD_DIM, zero, pair)
    return jnp.concatenate([first, second], 0).astype(bf16)


def join_heads(stacked):
    lane = lax.broadcasted_iota(jnp.int32, (BLOCK, PAIR), 1)
    return jnp.where(lane < HEAD_DIM, stacked[:BLOCK], stacked[BLOCK:])


def dot_last(left, right):
    return lax.dot_general(left, right, (((1,), (1,)), ((), ())), preferred_element_type=f32)


def dot_first(left, right):
    return lax.dot_general(left, right, (((0,), (0,)), ((), ())), preferred_element_type=f32)


def attention_kernel(
    edge_ref, q_ref, k_ref, v_ref, cos_ref, sin_ref, o_ref, p_ref, qo_ref, ko_ref, vo_ref
):
    blocks = o_ref.shape[0] // BLOCK
    for start in range(0, k_ref.shape[0], BLOCK):
        rows = pl.ds(start, BLOCK)
        raw = k_ref[rows, :]
        ko_ref[rows, :] = (raw * cos_ref[rows, :] + turn(raw) * sin_ref[rows, :]).astype(bf16)
        vo_ref[rows, :] = v_ref[rows, :].astype(bf16)
    row = lax.broadcasted_iota(jnp.int32, (2 * BLOCK, SPAN), 0) & (BLOCK - 1)
    column = lax.broadcasted_iota(jnp.int32, (2 * BLOCK, SPAN), 1)
    band = (column >= row) & (column - row <= 2 * WINDOW)
    for index in range(blocks):
        own = pl.ds(index * BLOCK, BLOCK)
        wide = pl.ds(index * BLOCK + WINDOW, BLOCK)
        keys = pl.ds(index * BLOCK, SPAN)
        raw = q_ref[wide, :]
        query = (raw * cos_ref[wide, :] + turn(raw) * sin_ref[wide, :]).astype(bf16)
        qo_ref[own, :] = query
        scores = dot_last(split_heads(query.astype(f32) * HEAD_DIM**-0.5), ko_ref[keys, :])
        valid = band
        if index == 0:
            valid = valid & (column >= edge_ref[0])
        if index == blocks - 1:
            valid = valid & (column < edge_ref[1])
        scores = jnp.where(valid, scores, masked_score)
        weights = jnp.exp(scores - jnp.max(scores, -1, keepdims=True))
        probs = (weights * (1.0 / jnp.sum(weights, -1, keepdims=True))).astype(bf16)
        p_ref[0, index] = probs
        mixed = jnp.dot(probs, vo_ref[keys, :], preferred_element_type=f32)
        o_ref[own, :] = join_heads(mixed).astype(bf16)


def attention_back_kernel(
    do_ref, q_ref, k_ref, v_ref, p_ref, cos_ref, sin_ref, dq_ref, dk_ref, dv_ref
):
    blocks = do_ref.shape[0] // BLOCK
    scale = HEAD_DIM**-0.5

    def turn_back(grad, rows):
        return (grad * cos_ref[rows, :] - turn(grad) * sin_ref[rows, :]).astype(bf16)

    dk_carry = dv_carry = jnp.zeros((BLOCK, PAIR), f32)
    for index in range(blocks):
        own = pl.ds(index * BLOCK, BLOCK)
        wide = pl.ds(index * BLOCK + WINDOW, BLOCK)
        keys = pl.ds(index * BLOCK, SPAN)
        grad = split_heads(do_ref[own, :].astype(f32))
        query = split_heads(q_ref[own, :].astype(f32) * scale)
        low = p_ref[0, index]
        probs = low.astype(f32)
        grad_probs = dot_last(grad, v_ref[keys, :])
        inner = jnp.sum(probs * grad_probs, -1, keepdims=True)
        grad_scores = (probs * (grad_probs - inner)).astype(bf16)
        dq = join_heads(jnp.dot(grad_scores, k_ref[keys, :], preferred_element_type=f32)) * scale
        dq_ref[own, :] = turn_back(dq, wide)
        dk_part = dot_first(grad_scores, query)
        dv_part = dot_first(low, grad)
        dk_ref[own, :] = turn_back(dk_carry + dk_part[:BLOCK], own)
        dv_ref[own, :] = (dv_carry + dv_part[:BLOCK]).astype(bf16)
        dk_carry, dv_carry = dk_part[BLOCK:], dv_part[BLOCK:]
    last = pl.ds(blocks * BLOCK, BLOCK)
    dk_ref[last, :] = turn_back(dk_carry, last)
    dv_ref[last, :] = dv_carry.astype(bf16)


def column_spec(rows, first=0):
    return pl.BlockSpec((rows, PAIR), lambda pair: (0, pair + first))


def attention(edges, projected, cosine, sine):
    wide = projected.shape[0]
    tokens = wide - 2 * WINDOW
    pairs = HEADS // 2
    blocks = tokens // BLOCK
    table = pl.BlockSpec((wide, PAIR), lambda pair: (0, 0))
    return pl.pallas_call(
        attention_kernel,
        grid=(pairs,),
        in_specs=[
            pl.BlockSpec(memory_space=pltpu.SMEM),
            column_spec(wide),
            column_spec(wide, pairs),
            column_spec(wide, 2 * pairs),
            table,
            table,
        ],
        out_specs=[
            column_spec(tokens),
            pl.BlockSpec((1, blocks, 2 * BLOCK, SPAN), lambda pair: (pair, 0, 0, 0)),
            column_spec(tokens),
            column_spec(wide),
            column_spec(wide),
        ],
        out_shape=[
            jax.ShapeDtypeStruct((tokens, D), bf16),
            jax.ShapeDtypeStruct((pairs, blocks, 2 * BLOCK, SPAN), bf16),
            jax.ShapeDtypeStruct((tokens, D), bf16),
            jax.ShapeDtypeStruct((wide, D), bf16),
            jax.ShapeDtypeStruct((wide, D), bf16),
        ],
        cost_estimate=pl.CostEstimate(
            flops=4 * D * tokens * SPAN, bytes_accessed=30_000_000, transcendentals=HEADS * tokens * SPAN
        ),
        compiler_params=pltpu.CompilerParams(vmem_limit_bytes=40 * 1024 * 1024),
        name="attention_forward",
    )(edges, projected, projected, projected, cosine, sine)


def attention_back(grad_mixed, query, key, value, probs, cosine, sine):
    wide = key.shape[0]
    tokens = wide - 2 * WINDOW
    pairs = HEADS // 2
    blocks = tokens // BLOCK
    table = pl.BlockSpec((wide, PAIR), lambda pair: (0, 0))
    return pl.pallas_call(
        attention_back_kernel,
        grid=(pairs,),
        in_specs=[
            column_spec(tokens),
            column_spec(tokens),
            column_spec(wide),
            column_spec(wide),
            pl.BlockSpec((1, blocks, 2 * BLOCK, SPAN), lambda pair: (pair, 0, 0, 0)),
            table,
            table,
        ],
        out_specs=[column_spec(tokens), column_spec(wide), column_spec(wide)],
        out_shape=[
            jax.ShapeDtypeStruct((tokens, D), bf16),
            jax.ShapeDtypeStruct((wide, D), bf16),
            jax.ShapeDtypeStruct((wide, D), bf16),
        ],
        cost_estimate=pl.CostEstimate(
            flops=8 * D * tokens * SPAN, bytes_accessed=20_000_000, transcendentals=0
        ),
        compiler_params=pltpu.CompilerParams(vmem_limit_bytes=40 * 1024 * 1024),
        name="attention_backward",
    )(grad_mixed, query, key, value, probs, cosine, sine)


def gather(weight):
    return lax.all_gather(weight, "dp", axis=0, tiled=True)


def scatter_sum(grad):
    share = lax.psum_scatter(grad.astype(bf16), "dp", scatter_dimension=0, tiled=True)
    return lax.psum(share, "seq").astype(f32)


def shards(inputs, attn_gain, qkv_weight, proj_weight, mlp_gain, in_weight, out_weight, cotangent):
    tokens = inputs.shape[0]
    seq_count = lax.axis_size("seq")
    place = lax.axis_index("seq")
    forward = [(i, i + 1) for i in range(seq_count - 1)]
    backward = [(i + 1, i) for i in range(seq_count - 1)]

    qkv_full = gather(qkv_weight)
    attn_full = gather(attn_gain).astype(f32)
    mlp_full = gather(mlp_gain).astype(f32)
    proj_full = gather(proj_weight)
    in_full = gather(in_weight)
    out_full = gather(out_weight)

    before = lax.ppermute(inputs[-WINDOW:], "seq", forward)
    after = lax.ppermute(inputs[:WINDOW], "seq", backward)
    x_wide = jnp.concatenate([before, inputs, after], 0).astype(f32)
    xhat_wide, scale_wide = norm_parts(x_wide)
    n1_wide = (xhat_wide * attn_full).astype(bf16)
    projected = jnp.dot(n1_wide, qkv_full, preferred_element_type=f32)
    positions = (place * tokens - WINDOW + jnp.arange(tokens + 2 * WINDOW, dtype=jnp.int32)).astype(
        f32
    )
    cosine, sine = rotary_tables(positions)
    edges = jnp.stack(
        [jnp.where(place == 0, WINDOW, 0), jnp.where(place == seq_count - 1, SPAN - WINDOW, SPAN)]
    ).astype(jnp.int32)
    mixed, probs, query, key, value = attention(edges, projected, cosine, sine)

    residual = inputs.astype(f32)
    hidden = residual + jnp.dot(mixed, proj_full, preferred_element_type=f32)
    xhat_two, scale_two = norm_parts(hidden)
    n2 = (xhat_two * mlp_full).astype(bf16)
    up = jnp.dot(n2, in_full, preferred_element_type=f32)
    a, g = up[:, :FF], up[:, FF:]
    cdf = 0.5 * (1.0 + lax.erf(a * (0.5**0.5)))
    gelu = a * cdf
    gelu_slope = cdf + a * (jnp.exp(-0.5 * a * a) * (0.5 / jnp.pi) ** 0.5)
    m = (gelu * g).astype(bf16)
    output = (hidden + jnp.dot(m, out_full, preferred_element_type=f32)).astype(bf16)

    out_grad = jnp.einsum("tf,td->fd", m, cotangent, preferred_element_type=f32)
    out_total = scatter_sum(out_grad)
    dm = jnp.einsum("td,fd->tf", cotangent, out_full, preferred_element_type=f32)
    du = jnp.concatenate([dm * g * gelu_slope, dm * gelu], 1).astype(bf16)
    in_grad = jnp.einsum("td,tf->df", n2, du, preferred_element_type=f32)
    in_total = scatter_sum(in_grad)
    dn2 = jnp.einsum("tf,df->td", du, in_full, preferred_element_type=f32)
    dh = cotangent.astype(f32) + norm_back(dn2 * mlp_full, xhat_two, scale_two)
    da = dh.astype(bf16)
    proj_grad = jnp.einsum("te,td->ed", mixed, da, preferred_element_type=f32)
    proj_total = scatter_sum(proj_grad)
    grad_mixed = jnp.einsum("td,ed->te", da, proj_full, preferred_element_type=f32).astype(bf16)

    dq, dk_wide, dv_wide = attention_back(grad_mixed, query, key, value, probs, cosine, sine)
    own = slice(WINDOW, WINDOW + tokens)
    kv_head = jnp.concatenate([dk_wide[:WINDOW], dv_wide[:WINDOW]], 1)
    kv_tail = jnp.concatenate([dk_wide[-WINDOW:], dv_wide[-WINDOW:]], 1)
    from_after = lax.ppermute(kv_head, "seq", backward)
    from_before = lax.ppermute(kv_tail, "seq", forward)
    qkv_grad = jnp.concatenate(
        [
            dot_first(n1_wide[own], dq).astype(bf16),
            dot_first(n1_wide, dk_wide).astype(bf16),
            dot_first(n1_wide, dv_wide).astype(bf16),
        ],
        1,
    )
    qkv_total = scatter_sum(qkv_grad)
    kv = jnp.concatenate([dk_wide[own], dv_wide[own]], 1)
    kv = jnp.concatenate(
        [
            (kv[:WINDOW].astype(f32) + from_before.astype(f32)).astype(bf16),
            kv[WINDOW:-WINDOW],
            (kv[-WINDOW:].astype(f32) + from_after.astype(f32)).astype(bf16),
        ],
        0,
    )
    dproj = jnp.concatenate([dq, kv], 1)
    dn1 = dot_last(dproj, qkv_full)
    xhat_one, scale_one = norm_parts(residual)
    input_grad = (dh + norm_back(dn1 * attn_full, xhat_one, scale_one)).astype(bf16)

    attn_gain_grad = jnp.sum(qkv_weight.astype(f32) * qkv_total, -1) / attn_gain.astype(f32)
    mlp_gain_grad = jnp.sum(in_weight.astype(f32) * in_total, -1) / mlp_gain.astype(f32)
    return (
        output,
        input_grad,
        attn_gain_grad,
        qkv_total,
        proj_total,
        mlp_gain_grad,
        in_total,
        out_total,
    )


def solution(mesh):
    rows, split = P(("dp", "seq"), None), P("dp", None)
    in_specs = (rows, P("dp"), split, split, P("dp"), split, split, rows)
    out_specs = (rows, rows, P("dp"), split, split, P("dp"), split, split)
    return jax.shard_map(shards, mesh=mesh, in_specs=in_specs, out_specs=out_specs, check_vma=False)
```

```python
import jax
import jax.numpy as jnp
from jax import lax
from jax.experimental import pallas as pl
from jax.experimental.pallas import tpu as pltpu
from jax.sharding import PartitionSpec as P

D = 768
HEADS = 12
HEAD_DIM = 64
FF = 1152
WINDOW = 64
BLOCK = 128
SPAN = BLOCK + 2 * WINDOW
PAIR = 2 * HEAD_DIM

epsilon = 1e-05
theta_base = 10000.0
masked_score = -1e30
bf16, f32 = jnp.bfloat16, jnp.float32


def norm_parts(features):
    center = features - jnp.mean(features, -1, keepdims=True)
    spread = jnp.mean(center * center, -1, keepdims=True)
    scale = lax.rsqrt(spread + epsilon)
    return center * scale, scale


def norm_back(grad, xhat, scale):
    return scale * (
        grad - jnp.mean(grad, -1, keepdims=True) - xhat * jnp.mean(grad * xhat, -1, keepdims=True)
    )


def rotary_tables(positions):
    half = HEAD_DIM // 2
    inverse_freq = theta_base ** (-(jnp.arange(half, dtype=f32) * 2.0) / HEAD_DIM)
    angles = positions[:, None] * inverse_freq[None, :]
    cosine, sine = jnp.cos(angles), jnp.sin(angles)
    return (
        jnp.concatenate([cosine, cosine, cosine, cosine], -1),
        jnp.concatenate([-sine, sine, -sine, sine], -1),
    )


def turn(values):
    lane = lax.broadcasted_iota(jnp.int32, values.shape, 1)
    low_half = (lane & (HEAD_DIM - 1)) < HEAD_DIM // 2
    return jnp.where(
        low_half,
        pltpu.roll(values, PAIR - HEAD_DIM // 2, 1),
        pltpu.roll(values, HEAD_DIM // 2, 1),
    )


def split_heads(pair):
    lane = lax.broadcasted_iota(jnp.int32, pair.shape, 1)
    zero = jnp.zeros_like(pair)
    first = jnp.where(lane < HEAD_DIM, pair, zero)
    second = jnp.where(lane < HEAD_DIM, zero, pair)
    return jnp.concatenate([first, second], 0).astype(bf16)


def join_heads(stacked):
    lane = lax.broadcasted_iota(jnp.int32, (BLOCK, PAIR), 1)
    return jnp.where(lane < HEAD_DIM, stacked[:BLOCK], stacked[BLOCK:])


def dot_last(left, right):
    return lax.dot_general(left, right, (((1,), (1,)), ((), ())), preferred_element_type=f32)


def dot_first(left, right):
    return lax.dot_general(left, right, (((0,), (0,)), ((), ())), preferred_element_type=f32)


def attention_kernel(
    edge_ref, q_ref, k_ref, v_ref, cos_ref, sin_ref, o_ref, p_ref, qo_ref, ko_ref, vo_ref
):
    blocks = o_ref.shape[0] // BLOCK
    for start in range(0, k_ref.shape[0], BLOCK):
        rows = pl.ds(start, BLOCK)
        raw = k_ref[rows, :]
        ko_ref[rows, :] = (raw * cos_ref[rows, :] + turn(raw) * sin_ref[rows, :]).astype(bf16)
        vo_ref[rows, :] = v_ref[rows, :].astype(bf16)
    row = lax.broadcasted_iota(jnp.int32, (2 * BLOCK, SPAN), 0) & (BLOCK - 1)
    column = lax.broadcasted_iota(jnp.int32, (2 * BLOCK, SPAN), 1)
    band = (column >= row) & (column - row <= 2 * WINDOW)
    for index in range(blocks):
        own = pl.ds(index * BLOCK, BLOCK)
        wide = pl.ds(index * BLOCK + WINDOW, BLOCK)
        keys = pl.ds(index * BLOCK, SPAN)
        raw = q_ref[wide, :]
        query = (raw * cos_ref[wide, :] + turn(raw) * sin_ref[wide, :]).astype(bf16)
        qo_ref[own, :] = query
        scores = dot_last(split_heads(query.astype(f32) * HEAD_DIM**-0.5), ko_ref[keys, :])
        valid = band
        if index == 0:
            valid = valid & (column >= edge_ref[0])
        if index == blocks - 1:
            valid = valid & (column < edge_ref[1])
        scores = jnp.where(valid, scores, masked_score)
        weights = jnp.exp(scores - jnp.max(scores, -1, keepdims=True))
        probs = (weights * (1.0 / jnp.sum(weights, -1, keepdims=True))).astype(bf16)
        p_ref[0, index] = probs
        mixed = jnp.dot(probs, vo_ref[keys, :], preferred_element_type=f32)
        o_ref[own, :] = join_heads(mixed).astype(bf16)


def attention_back_kernel(
    do_ref, q_ref, k_ref, v_ref, p_ref, cos_ref, sin_ref, dq_ref, dk_ref, dv_ref
):
    blocks = do_ref.shape[0] // BLOCK
    scale = HEAD_DIM**-0.5

    def turn_back(grad, rows):
        return (grad * cos_ref[rows, :] - turn(grad) * sin_ref[rows, :]).astype(bf16)

    dk_carry = dv_carry = jnp.zeros((BLOCK, PAIR), f32)
    for index in range(blocks):
        own = pl.ds(index * BLOCK, BLOCK)
        wide = pl.ds(index * BLOCK + WINDOW, BLOCK)
        keys = pl.ds(index * BLOCK, SPAN)
        grad = split_heads(do_ref[own, :].astype(f32))
        query = split_heads(q_ref[own, :].astype(f32) * scale)
        low = p_ref[0, index]
        probs = low.astype(f32)
        grad_probs = dot_last(grad, v_ref[keys, :])
        inner = jnp.sum(probs * grad_probs, -1, keepdims=True)
        grad_scores = (probs * (grad_probs - inner)).astype(bf16)
        dq = join_heads(jnp.dot(grad_scores, k_ref[keys, :], preferred_element_type=f32)) * scale
        dq_ref[own, :] = turn_back(dq, wide)
        dk_part = dot_first(grad_scores, query)
        dv_part = dot_first(low, grad)
        dk_ref[own, :] = turn_back(dk_carry + dk_part[:BLOCK], own)
        dv_ref[own, :] = (dv_carry + dv_part[:BLOCK]).astype(bf16)
        dk_carry, dv_carry = dk_part[BLOCK:], dv_part[BLOCK:]
    last = pl.ds(blocks * BLOCK, BLOCK)
    dk_ref[last, :] = turn_back(dk_carry, last)
    dv_ref[last, :] = dv_carry.astype(bf16)


def column_spec(rows, first=0):
    return pl.BlockSpec((rows, PAIR), lambda pair: (0, pair + first))


def attention(edges, projected, cosine, sine):
    wide = projected.shape[0]
    tokens = wide - 2 * WINDOW
    pairs = HEADS // 2
    blocks = tokens // BLOCK
    table = pl.BlockSpec((wide, PAIR), lambda pair: (0, 0))
    return pl.pallas_call(
        attention_kernel,
        grid=(pairs,),
        in_specs=[
            pl.BlockSpec(memory_space=pltpu.SMEM),
            column_spec(wide),
            column_spec(wide, pairs),
            column_spec(wide, 2 * pairs),
            table,
            table,
        ],
        out_specs=[
            column_spec(tokens),
            pl.BlockSpec((1, blocks, 2 * BLOCK, SPAN), lambda pair: (pair, 0, 0, 0)),
            column_spec(tokens),
            column_spec(wide),
            column_spec(wide),
        ],
        out_shape=[
            jax.ShapeDtypeStruct((tokens, D), bf16),
            jax.ShapeDtypeStruct((pairs, blocks, 2 * BLOCK, SPAN), bf16),
            jax.ShapeDtypeStruct((tokens, D), bf16),
            jax.ShapeDtypeStruct((wide, D), bf16),
            jax.ShapeDtypeStruct((wide, D), bf16),
        ],
        cost_estimate=pl.CostEstimate(
            flops=4 * D * tokens * SPAN, bytes_accessed=30_000_000, transcendentals=HEADS * tokens * SPAN
        ),
        compiler_params=pltpu.CompilerParams(vmem_limit_bytes=40 * 1024 * 1024),
        name="attention_forward",
    )(edges, projected, projected, projected, cosine, sine)


def attention_back(grad_mixed, query, key, value, probs, cosine, sine):
    wide = key.shape[0]
    tokens = wide - 2 * WINDOW
    pairs = HEADS // 2
    blocks = tokens // BLOCK
    table = pl.BlockSpec((wide, PAIR), lambda pair: (0, 0))
    return pl.pallas_call(
        attention_back_kernel,
        grid=(pairs,),
        in_specs=[
            column_spec(tokens),
            column_spec(tokens),
            column_spec(wide),
            column_spec(wide),
            pl.BlockSpec((1, blocks, 2 * BLOCK, SPAN), lambda pair: (pair, 0, 0, 0)),
            table,
            table,
        ],
        out_specs=[column_spec(tokens), column_spec(wide), column_spec(wide)],
        out_shape=[
            jax.ShapeDtypeStruct((tokens, D), bf16),
            jax.ShapeDtypeStruct((wide, D), bf16),
            jax.ShapeDtypeStruct((wide, D), bf16),
        ],
        cost_estimate=pl.CostEstimate(
            flops=8 * D * tokens * SPAN, bytes_accessed=20_000_000, transcendentals=0
        ),
        compiler_params=pltpu.CompilerParams(vmem_limit_bytes=40 * 1024 * 1024),
        name="attention_backward",
    )(grad_mixed, query, key, value, probs, cosine, sine)


def gather(weight):
    return lax.all_gather(weight, "dp", axis=0, tiled=True)


def bit_of(place, bit):
    return lax.rem(place // 2**bit, 2)


def partner(place, bit):
    return place + (1 - 2 * bit_of(place, bit)) * 2**bit


def reduce_kernel(count, dp_bits, seq_bits, *refs):
    grads, outs, scratch = refs[:count], refs[count : 2 * count], refs[2 * count :]
    send_sems, recv_sems = scratch[-2:]
    buffers = iter(scratch[:-2])
    me, place = lax.axis_index("dp"), lax.axis_index("seq")
    dp_size = 2**dp_bits
    parts = [(array, stream) for array in range(count) for stream in range(2)]
    orders = (
        list(range(dp_bits)),
        [0] + list(range(dp_bits - 1, 0, -1)),
    )
    received, summed = {}, {}
    for array, stream in parts:
        for step in range(dp_bits):
            received[array, stream, step] = next(buffers)
            if step < dp_bits - 1:
                summed[array, stream, step] = next(buffers)
    shares = [next(buffers) for _ in range(count)]
    seq_received = [[next(buffers) for _ in range(seq_bits)] for _ in range(count)]
    seq_summed = [[next(buffers) for _ in range(seq_bits - 1)] for _ in range(count)]
    totals = [next(buffers) for _ in range(count)]

    barrier = pltpu.get_barrier_semaphore()
    for bit in range(dp_bits):
        pl.semaphore_signal(
            barrier, inc=1, device_id={"dp": partner(me, bit)}, device_id_type=pl.DeviceIdType.MESH
        )
    for bit in range(seq_bits):
        pl.semaphore_signal(
            barrier,
            inc=1,
            device_id={"seq": partner(place, bit)},
            device_id_type=pl.DeviceIdType.MESH,
        )
    pl.semaphore_wait(barrier, dp_bits + seq_bits)

    used = [0]

    def send(source, target, device):
        number = used[0]
        used[0] += 1
        copy = pltpu.make_async_remote_copy(
            src_ref=source,
            dst_ref=target,
            send_sem=send_sems.at[number],
            recv_sem=recv_sems.at[number],
            device_id=device,
            device_id_type=pl.DeviceIdType.MESH,
        )
        copy.start()
        return copy

    def columns(array, stream):
        half = grads[array].shape[2] // 2
        return pl.ds(stream * half, half)

    def block_of(order, own, slot):
        block = own
        for level, bit in enumerate(order[1:]):
            block = block + ((slot >> (dp_bits - 2 - level)) & 1) * 2**bit
        return block

    def add(left, right):
        return (left.astype(f32) + right.astype(f32)).astype(bf16)

    pending = {}
    half_blocks = dp_size // 2
    for array, stream in parts:
        order = orders[stream]
        first = order[0]
        theirs = (1 - bit_of(me, first)) * 2**first
        pending[array, stream] = [
            send(
                grads[array].at[block_of(order, theirs, slot), :, columns(array, stream)],
                received[array, stream, 0].at[slot],
                {"dp": partner(me, first)},
            )
            for slot in range(half_blocks)
        ]
    for step in range(dp_bits):
        width = half_blocks >> step
        for array, stream in parts:
            order = orders[stream]
            last = step == dp_bits - 1
            for slot in range(width):
                if step == 0:
                    mine = bit_of(me, order[0]) * 2 ** order[0]
                    kept = grads[array][block_of(order, mine, slot), :, columns(array, stream)]
                    pending[array, stream][slot].wait()
                else:
                    if slot == 0:
                        pending[array, stream][0].wait()
                    kept = summed[array, stream, step - 1][bit_of(me, order[step]) * width + slot]
                value = add(kept, received[array, stream, step][slot])
                if last:
                    shares[array][stream] = value
                else:
                    summed[array, stream, step][slot] = value
            if not last:
                bit = order[step + 1]
                away = (1 - bit_of(me, bit)) * (width // 2)
                pending[array, stream] = [
                    send(
                        summed[array, stream, step].at[pl.ds(away, width // 2)],
                        received[array, stream, step + 1],
                        {"dp": partner(me, bit)},
                    )
                ]
    side = bit_of(place, 0)
    neighbour = {"seq": partner(place, 0)}
    copies = [
        send(shares[array].at[1 - side], seq_received[array][0], neighbour)
        for array in range(count)
    ]
    for bit in range(seq_bits):
        for array in range(count):
            copies[array].wait()
            kept = shares[array][side] if bit == 0 else seq_summed[array][bit - 1][...]
            value = add(kept, seq_received[array][bit][...])
            if bit < seq_bits - 1:
                seq_summed[array][bit][...] = value
                copies[array] = send(
                    seq_summed[array][bit],
                    seq_received[array][bit + 1],
                    {"seq": partner(place, bit + 1)},
                )
            else:
                totals[array][side] = value
                copies[array] = send(
                    totals[array].at[side], totals[array].at[side], neighbour
                )
    for array in range(count):
        copies[array].wait()
        for stream in range(2):
            outs[array][:, columns(array, stream)] = totals[array][stream].astype(f32)


def reduce_all(grads, collective):
    dp_size, seq_size = lax.axis_size("dp"), lax.axis_size("seq")
    dp_bits, seq_bits = dp_size.bit_length() - 1, seq_size.bit_length() - 1
    count = len(grads)
    blocks = [grad.astype(bf16).reshape(dp_size, -1, grad.shape[1]) for grad in grads]
    scratch = []
    halves = [(block.shape[1], block.shape[2] // 2) for block in blocks]
    for half in halves:
        for _ in range(2):
            for step in range(dp_bits):
                width = (dp_size // 2) >> step
                scratch.append(pltpu.VMEM((width,) + half, bf16))
                if step < dp_bits - 1:
                    scratch.append(pltpu.VMEM((width,) + half, bf16))
    scratch += [pltpu.VMEM((2,) + half, bf16) for half in halves]
    scratch += [pltpu.VMEM(half, bf16) for half in halves for _ in range(seq_bits)]
    scratch += [pltpu.VMEM(half, bf16) for half in halves for _ in range(seq_bits - 1)]
    scratch += [pltpu.VMEM((2,) + half, bf16) for half in halves]
    total = count * (2 * (dp_size // 2 + dp_bits - 1) + seq_bits + 1)
    scratch += [pltpu.SemaphoreType.DMA((total,)), pltpu.SemaphoreType.DMA((total,))]

    def body(*refs):
        reduce_kernel(count, dp_bits, seq_bits, *refs)

    return pl.pallas_call(
        body,
        in_specs=[pl.BlockSpec(memory_space=pltpu.VMEM)] * count,
        out_specs=[pl.BlockSpec(memory_space=pltpu.VMEM)] * count,
        out_shape=[jax.ShapeDtypeStruct(block.shape[1:], f32) for block in blocks],
        scratch_shapes=scratch,
        compiler_params=pltpu.CompilerParams(
            collective_id=collective, has_side_effects=True, vmem_limit_bytes=56 * 1024 * 1024
        ),
        name="gradient_sums",
    )(*blocks)


def shards(inputs, attn_gain, qkv_weight, proj_weight, mlp_gain, in_weight, out_weight, cotangent):
    tokens = inputs.shape[0]
    seq_count = lax.axis_size("seq")
    place = lax.axis_index("seq")
    forward = [(i, i + 1) for i in range(seq_count - 1)]
    backward = [(i + 1, i) for i in range(seq_count - 1)]

    qkv_full = gather(qkv_weight)
    attn_full = gather(attn_gain).astype(f32)
    mlp_full = gather(mlp_gain).astype(f32)
    proj_full = gather(proj_weight)
    in_full = gather(in_weight)
    out_full = gather(out_weight)

    before = lax.ppermute(inputs[-WINDOW:], "seq", forward)
    after = lax.ppermute(inputs[:WINDOW], "seq", backward)
    x_wide = jnp.concatenate([before, inputs, after], 0).astype(f32)
    xhat_wide, scale_wide = norm_parts(x_wide)
    n1_wide = (xhat_wide * attn_full).astype(bf16)
    projected = jnp.dot(n1_wide, qkv_full, preferred_element_type=f32)
    positions = (place * tokens - WINDOW + jnp.arange(tokens + 2 * WINDOW, dtype=jnp.int32)).astype(
        f32
    )
    cosine, sine = rotary_tables(positions)
    edges = jnp.stack(
        [jnp.where(place == 0, WINDOW, 0), jnp.where(place == seq_count - 1, SPAN - WINDOW, SPAN)]
    ).astype(jnp.int32)
    mixed, probs, query, key, value = attention(edges, projected, cosine, sine)

    residual = inputs.astype(f32)
    hidden = residual + jnp.dot(mixed, proj_full, preferred_element_type=f32)
    xhat_two, scale_two = norm_parts(hidden)
    n2 = (xhat_two * mlp_full).astype(bf16)
    up = jnp.dot(n2, in_full, preferred_element_type=f32)
    a, g = up[:, :FF], up[:, FF:]
    cdf = 0.5 * (1.0 + lax.erf(a * (0.5**0.5)))
    gelu = a * cdf
    gelu_slope = cdf + a * (jnp.exp(-0.5 * a * a) * (0.5 / jnp.pi) ** 0.5)
    m = (gelu * g).astype(bf16)
    output = (hidden + jnp.dot(m, out_full, preferred_element_type=f32)).astype(bf16)

    out_grad = jnp.einsum("tf,td->fd", m, cotangent, preferred_element_type=f32)
    dm = jnp.einsum("td,fd->tf", cotangent, out_full, preferred_element_type=f32)
    du = jnp.concatenate([dm * g * gelu_slope, dm * gelu], 1).astype(bf16)
    in_grad = jnp.einsum("td,tf->df", n2, du, preferred_element_type=f32)
    dn2 = jnp.einsum("tf,df->td", du, in_full, preferred_element_type=f32)
    dh = cotangent.astype(f32) + norm_back(dn2 * mlp_full, xhat_two, scale_two)
    da = dh.astype(bf16)
    proj_grad = jnp.einsum("te,td->ed", mixed, da, preferred_element_type=f32)
    grad_mixed = jnp.einsum("td,ed->te", da, proj_full, preferred_element_type=f32).astype(bf16)

    dq, dk_wide, dv_wide = attention_back(grad_mixed, query, key, value, probs, cosine, sine)
    own = slice(WINDOW, WINDOW + tokens)
    kv_head = jnp.concatenate([dk_wide[:WINDOW], dv_wide[:WINDOW]], 1)
    kv_tail = jnp.concatenate([dk_wide[-WINDOW:], dv_wide[-WINDOW:]], 1)
    from_after = lax.ppermute(kv_head, "seq", backward)
    from_before = lax.ppermute(kv_tail, "seq", forward)
    qkv_grad = jnp.concatenate(
        [
            dot_first(n1_wide[own], dq).astype(bf16),
            dot_first(n1_wide, dk_wide).astype(bf16),
            dot_first(n1_wide, dv_wide).astype(bf16),
        ],
        1,
    )
    kv = jnp.concatenate([dk_wide[own], dv_wide[own]], 1)
    kv = jnp.concatenate(
        [
            (kv[:WINDOW].astype(f32) + from_before.astype(f32)).astype(bf16),
            kv[WINDOW:-WINDOW],
            (kv[-WINDOW:].astype(f32) + from_after.astype(f32)).astype(bf16),
        ],
        0,
    )
    dproj = jnp.concatenate([dq, kv], 1)
    dn1 = dot_last(dproj, qkv_full)
    xhat_one, scale_one = norm_parts(residual)
    input_grad = (dh + norm_back(dn1 * attn_full, xhat_one, scale_one)).astype(bf16)

    out_total, in_total, proj_total, qkv_total = reduce_all(
        [out_grad, in_grad, proj_grad, qkv_grad], 1
    )
    attn_gain_grad = jnp.sum(qkv_weight.astype(f32) * qkv_total, -1) / attn_gain.astype(f32)
    mlp_gain_grad = jnp.sum(in_weight.astype(f32) * in_total, -1) / mlp_gain.astype(f32)
    return (
        output,
        input_grad,
        attn_gain_grad,
        qkv_total,
        proj_total,
        mlp_gain_grad,
        in_total,
        out_total,
    )


def solution(mesh):
    rows, split = P(("dp", "seq"), None), P("dp", None)
    in_specs = (rows, P("dp"), split, split, P("dp"), split, split, rows)
    out_specs = (rows, rows, P("dp"), split, split, P("dp"), split, split)
    return jax.shard_map(shards, mesh=mesh, in_specs=in_specs, out_specs=out_specs, check_vma=False)
```

```python
import jax
import jax.numpy as jnp
from jax import lax
from jax.experimental import pallas as pl
from jax.experimental.pallas import tpu as pltpu
from jax.sharding import PartitionSpec as P

D = 768
HEADS = 12
HEAD_DIM = 64
FF = 1152
WINDOW = 64
BLOCK = 128
SPAN = BLOCK + 2 * WINDOW
PAIR = 2 * HEAD_DIM

epsilon = 1e-05
theta_base = 10000.0
masked_score = -1e30
bf16, f32 = jnp.bfloat16, jnp.float32


def norm_parts(features):
    center = features - jnp.mean(features, -1, keepdims=True)
    spread = jnp.mean(center * center, -1, keepdims=True)
    scale = lax.rsqrt(spread + epsilon)
    return center * scale, scale


def norm_back(grad, xhat, scale):
    return scale * (
        grad - jnp.mean(grad, -1, keepdims=True) - xhat * jnp.mean(grad * xhat, -1, keepdims=True)
    )


def rotary_tables(positions):
    half = HEAD_DIM // 2
    inverse_freq = theta_base ** (-(jnp.arange(half, dtype=f32) * 2.0) / HEAD_DIM)
    angles = positions[:, None] * inverse_freq[None, :]
    cosine, sine = jnp.cos(angles), jnp.sin(angles)
    return (
        jnp.concatenate([cosine, cosine, cosine, cosine], -1),
        jnp.concatenate([-sine, sine, -sine, sine], -1),
    )


def turn(values):
    lane = lax.broadcasted_iota(jnp.int32, values.shape, 1)
    low_half = (lane & (HEAD_DIM - 1)) < HEAD_DIM // 2
    return jnp.where(
        low_half,
        pltpu.roll(values, PAIR - HEAD_DIM // 2, 1),
        pltpu.roll(values, HEAD_DIM // 2, 1),
    )


def split_heads(pair):
    lane = lax.broadcasted_iota(jnp.int32, pair.shape, 1)
    zero = jnp.zeros_like(pair)
    first = jnp.where(lane < HEAD_DIM, pair, zero)
    second = jnp.where(lane < HEAD_DIM, zero, pair)
    return jnp.concatenate([first, second], 0).astype(bf16)


def join_heads(stacked):
    lane = lax.broadcasted_iota(jnp.int32, (BLOCK, PAIR), 1)
    return jnp.where(lane < HEAD_DIM, stacked[:BLOCK], stacked[BLOCK:])


def dot_last(left, right):
    return lax.dot_general(left, right, (((1,), (1,)), ((), ())), preferred_element_type=f32)


def dot_first(left, right):
    return lax.dot_general(left, right, (((0,), (0,)), ((), ())), preferred_element_type=f32)


def attention_kernel(
    edge_ref, q_ref, k_ref, v_ref, cos_ref, sin_ref, o_ref, p_ref, qo_ref, ko_ref, vo_ref
):
    blocks = o_ref.shape[0] // BLOCK
    for start in range(0, k_ref.shape[0], BLOCK):
        rows = pl.ds(start, BLOCK)
        raw = k_ref[rows, :]
        ko_ref[rows, :] = (raw * cos_ref[rows, :] + turn(raw) * sin_ref[rows, :]).astype(bf16)
        vo_ref[rows, :] = v_ref[rows, :].astype(bf16)
    row = lax.broadcasted_iota(jnp.int32, (2 * BLOCK, SPAN), 0) & (BLOCK - 1)
    column = lax.broadcasted_iota(jnp.int32, (2 * BLOCK, SPAN), 1)
    band = (column >= row) & (column - row <= 2 * WINDOW)
    for index in range(blocks):
        own = pl.ds(index * BLOCK, BLOCK)
        wide = pl.ds(index * BLOCK + WINDOW, BLOCK)
        keys = pl.ds(index * BLOCK, SPAN)
        raw = q_ref[wide, :]
        query = (raw * cos_ref[wide, :] + turn(raw) * sin_ref[wide, :]).astype(bf16)
        qo_ref[own, :] = query
        scores = dot_last(split_heads(query.astype(f32) * HEAD_DIM**-0.5), ko_ref[keys, :])
        valid = band
        if index == 0:
            valid = valid & (column >= edge_ref[0])
        if index == blocks - 1:
            valid = valid & (column < edge_ref[1])
        scores = jnp.where(valid, scores, masked_score)
        weights = jnp.exp(scores - jnp.max(scores, -1, keepdims=True))
        probs = (weights * (1.0 / jnp.sum(weights, -1, keepdims=True))).astype(bf16)
        p_ref[0, index] = probs
        mixed = jnp.dot(probs, vo_ref[keys, :], preferred_element_type=f32)
        o_ref[own, :] = join_heads(mixed).astype(bf16)


def attention_back_kernel(
    do_ref, q_ref, k_ref, v_ref, p_ref, cos_ref, sin_ref, dq_ref, dk_ref, dv_ref
):
    blocks = do_ref.shape[0] // BLOCK
    scale = HEAD_DIM**-0.5

    def turn_back(grad, rows):
        return (grad * cos_ref[rows, :] - turn(grad) * sin_ref[rows, :]).astype(bf16)

    dk_carry = dv_carry = jnp.zeros((BLOCK, PAIR), f32)
    for index in range(blocks):
        own = pl.ds(index * BLOCK, BLOCK)
        wide = pl.ds(index * BLOCK + WINDOW, BLOCK)
        keys = pl.ds(index * BLOCK, SPAN)
        grad = split_heads(do_ref[own, :].astype(f32))
        query = split_heads(q_ref[own, :].astype(f32) * scale)
        low = p_ref[0, index]
        probs = low.astype(f32)
        grad_probs = dot_last(grad, v_ref[keys, :])
        inner = jnp.sum(probs * grad_probs, -1, keepdims=True)
        grad_scores = (probs * (grad_probs - inner)).astype(bf16)
        dq = join_heads(jnp.dot(grad_scores, k_ref[keys, :], preferred_element_type=f32)) * scale
        dq_ref[own, :] = turn_back(dq, wide)
        dk_part = dot_first(grad_scores, query)
        dv_part = dot_first(low, grad)
        dk_ref[own, :] = turn_back(dk_carry + dk_part[:BLOCK], own)
        dv_ref[own, :] = (dv_carry + dv_part[:BLOCK]).astype(bf16)
        dk_carry, dv_carry = dk_part[BLOCK:], dv_part[BLOCK:]
    last = pl.ds(blocks * BLOCK, BLOCK)
    dk_ref[last, :] = turn_back(dk_carry, last)
    dv_ref[last, :] = dv_carry.astype(bf16)


def column_spec(rows, first=0):
    return pl.BlockSpec((rows, PAIR), lambda pair: (0, pair + first))


def attention(edges, projected, cosine, sine):
    wide = projected.shape[0]
    tokens = wide - 2 * WINDOW
    pairs = HEADS // 2
    blocks = tokens // BLOCK
    table = pl.BlockSpec((wide, PAIR), lambda pair: (0, 0))
    return pl.pallas_call(
        attention_kernel,
        grid=(pairs,),
        in_specs=[
            pl.BlockSpec(memory_space=pltpu.SMEM),
            column_spec(wide),
            column_spec(wide, pairs),
            column_spec(wide, 2 * pairs),
            table,
            table,
        ],
        out_specs=[
            column_spec(tokens),
            pl.BlockSpec((1, blocks, 2 * BLOCK, SPAN), lambda pair: (pair, 0, 0, 0)),
            column_spec(tokens),
            column_spec(wide),
            column_spec(wide),
        ],
        out_shape=[
            jax.ShapeDtypeStruct((tokens, D), bf16),
            jax.ShapeDtypeStruct((pairs, blocks, 2 * BLOCK, SPAN), bf16),
            jax.ShapeDtypeStruct((tokens, D), bf16),
            jax.ShapeDtypeStruct((wide, D), bf16),
            jax.ShapeDtypeStruct((wide, D), bf16),
        ],
        cost_estimate=pl.CostEstimate(
            flops=4 * D * tokens * SPAN, bytes_accessed=30_000_000, transcendentals=HEADS * tokens * SPAN
        ),
        compiler_params=pltpu.CompilerParams(vmem_limit_bytes=40 * 1024 * 1024),
        name="attention_forward",
    )(edges, projected, projected, projected, cosine, sine)


def attention_back(grad_mixed, query, key, value, probs, cosine, sine):
    wide = key.shape[0]
    tokens = wide - 2 * WINDOW
    pairs = HEADS // 2
    blocks = tokens // BLOCK
    table = pl.BlockSpec((wide, PAIR), lambda pair: (0, 0))
    return pl.pallas_call(
        attention_back_kernel,
        grid=(pairs,),
        in_specs=[
            column_spec(tokens),
            column_spec(tokens),
            column_spec(wide),
            column_spec(wide),
            pl.BlockSpec((1, blocks, 2 * BLOCK, SPAN), lambda pair: (pair, 0, 0, 0)),
            table,
            table,
        ],
        out_specs=[column_spec(tokens), column_spec(wide), column_spec(wide)],
        out_shape=[
            jax.ShapeDtypeStruct((tokens, D), bf16),
            jax.ShapeDtypeStruct((wide, D), bf16),
            jax.ShapeDtypeStruct((wide, D), bf16),
        ],
        cost_estimate=pl.CostEstimate(
            flops=8 * D * tokens * SPAN, bytes_accessed=20_000_000, transcendentals=0
        ),
        compiler_params=pltpu.CompilerParams(vmem_limit_bytes=40 * 1024 * 1024),
        name="attention_backward",
    )(grad_mixed, query, key, value, probs, cosine, sine)


def gather(weight):
    return lax.all_gather(weight, "dp", axis=0, tiled=True)


def bit_of(place, bit):
    return lax.rem(place // 2**bit, 2)


def partner(place, bit):
    return place + (1 - 2 * bit_of(place, bit)) * 2**bit


def reduce_kernel(count, dp_bits, seq_bits, *refs):
    grads, outs, scratch = refs[:count], refs[count : 2 * count], refs[2 * count :]
    send_sems, recv_sems = scratch[-2:]
    buffers = iter(scratch[:-2])
    me, place = lax.axis_index("dp"), lax.axis_index("seq")
    dp_size = 2**dp_bits
    parts = [(array, stream) for array in range(count) for stream in range(2)]
    orders = (
        list(range(dp_bits)),
        [0] + list(range(dp_bits - 1, 0, -1)),
    )
    received, summed = {}, {}
    for array, stream in parts:
        for step in range(dp_bits):
            received[array, stream, step] = next(buffers)
            if step < dp_bits - 1:
                summed[array, stream, step] = next(buffers)
    shares = [next(buffers) for _ in range(count)]
    seq_received = [[next(buffers) for _ in range(seq_bits)] for _ in range(count)]
    seq_summed = [[next(buffers) for _ in range(seq_bits - 1)] for _ in range(count)]
    totals = [next(buffers) for _ in range(count)]

    barrier = pltpu.get_barrier_semaphore()
    for bit in range(dp_bits):
        pl.semaphore_signal(
            barrier, inc=1, device_id={"dp": partner(me, bit)}, device_id_type=pl.DeviceIdType.MESH
        )
    for bit in range(seq_bits):
        pl.semaphore_signal(
            barrier,
            inc=1,
            device_id={"seq": partner(place, bit)},
            device_id_type=pl.DeviceIdType.MESH,
        )
    pl.semaphore_wait(barrier, dp_bits + seq_bits)

    used = [0]

    def send(source, target, device):
        number = used[0]
        used[0] += 1
        copy = pltpu.make_async_remote_copy(
            src_ref=source,
            dst_ref=target,
            send_sem=send_sems.at[number],
            recv_sem=recv_sems.at[number],
            device_id=device,
            device_id_type=pl.DeviceIdType.MESH,
        )
        copy.start()
        return copy

    def columns(array, stream):
        half = grads[array].shape[2] // 2
        return pl.ds(stream * half, half)

    def block_of(order, own, slot):
        block = own
        for level, bit in enumerate(order[1:]):
            block = block + ((slot >> (dp_bits - 2 - level)) & 1) * 2**bit
        return block

    def add(left, right):
        return (left.astype(f32) + right.astype(f32)).astype(bf16)

    pending = {}
    half_blocks = dp_size // 2
    for array, stream in parts:
        order = orders[stream]
        first = order[0]
        theirs = (1 - bit_of(me, first)) * 2**first
        pending[array, stream] = [
            send(
                grads[array].at[block_of(order, theirs, slot), :, columns(array, stream)],
                received[array, stream, 0].at[slot],
                {"dp": partner(me, first)},
            )
            for slot in range(half_blocks)
        ]
    for step in range(dp_bits):
        width = half_blocks >> step
        for array, stream in parts:
            order = orders[stream]
            last = step == dp_bits - 1
            for slot in range(width):
                if step == 0:
                    mine = bit_of(me, order[0]) * 2 ** order[0]
                    kept = grads[array][block_of(order, mine, slot), :, columns(array, stream)]
                    pending[array, stream][slot].wait()
                else:
                    if slot == 0:
                        pending[array, stream][0].wait()
                    kept = summed[array, stream, step - 1][bit_of(me, order[step]) * width + slot]
                value = add(kept, received[array, stream, step][slot])
                if last:
                    shares[array][stream] = value
                else:
                    summed[array, stream, step][slot] = value
            if not last:
                bit = order[step + 1]
                away = (1 - bit_of(me, bit)) * (width // 2)
                pending[array, stream] = [
                    send(
                        summed[array, stream, step].at[pl.ds(away, width // 2)],
                        received[array, stream, step + 1],
                        {"dp": partner(me, bit)},
                    )
                ]
    side = bit_of(place, 0)
    neighbour = {"seq": partner(place, 0)}
    copies = [
        send(shares[array].at[1 - side], seq_received[array][0], neighbour)
        for array in range(count)
    ]
    for bit in range(seq_bits):
        for array in range(count):
            copies[array].wait()
            kept = shares[array][side] if bit == 0 else seq_summed[array][bit - 1][...]
            value = add(kept, seq_received[array][bit][...])
            if bit < seq_bits - 1:
                seq_summed[array][bit][...] = value
                copies[array] = send(
                    seq_summed[array][bit],
                    seq_received[array][bit + 1],
                    {"seq": partner(place, bit + 1)},
                )
            else:
                totals[array][side] = value
                copies[array] = send(
                    totals[array].at[side], totals[array].at[side], neighbour
                )
    for array in range(count):
        copies[array].wait()
        for stream in range(2):
            outs[array][:, columns(array, stream)] = totals[array][stream].astype(f32)


def reduce_all(grads, collective):
    dp_size, seq_size = lax.axis_size("dp"), lax.axis_size("seq")
    dp_bits, seq_bits = dp_size.bit_length() - 1, seq_size.bit_length() - 1
    count = len(grads)
    blocks = [grad.astype(bf16).reshape(dp_size, -1, grad.shape[1]) for grad in grads]
    scratch = []
    halves = [(block.shape[1], block.shape[2] // 2) for block in blocks]
    for half in halves:
        for _ in range(2):
            for step in range(dp_bits):
                width = (dp_size // 2) >> step
                scratch.append(pltpu.VMEM((width,) + half, bf16))
                if step < dp_bits - 1:
                    scratch.append(pltpu.VMEM((width,) + half, bf16))
    scratch += [pltpu.VMEM((2,) + half, bf16) for half in halves]
    scratch += [pltpu.VMEM(half, bf16) for half in halves for _ in range(seq_bits)]
    scratch += [pltpu.VMEM(half, bf16) for half in halves for _ in range(seq_bits - 1)]
    scratch += [pltpu.VMEM((2,) + half, bf16) for half in halves]
    total = count * (2 * (dp_size // 2 + dp_bits - 1) + seq_bits + 1)
    scratch += [pltpu.SemaphoreType.DMA((total,)), pltpu.SemaphoreType.DMA((total,))]

    def body(*refs):
        reduce_kernel(count, dp_bits, seq_bits, *refs)

    return pl.pallas_call(
        body,
        in_specs=[pl.BlockSpec(memory_space=pltpu.VMEM)] * count,
        out_specs=[pl.BlockSpec(memory_space=pltpu.VMEM)] * count,
        out_shape=[jax.ShapeDtypeStruct(block.shape[1:], f32) for block in blocks],
        scratch_shapes=scratch,
        compiler_params=pltpu.CompilerParams(
            collective_id=collective, has_side_effects=True, vmem_limit_bytes=56 * 1024 * 1024
        ),
        name="gradient_sums",
    )(*blocks)

def gather_kernel(count, dp_bits, *refs):
    blocks, outs = refs[:count], refs[count : 2 * count]
    send_sems, recv_sems, own_sems = refs[2 * count :]
    me = lax.axis_index("dp")
    orders = (
        list(range(1, dp_bits)) + [0],
        list(range(dp_bits - 1, 0, -1)) + [0],
    )
    parts = [(array, stream) for array in range(count) for stream in range(2)]
    barrier = pltpu.get_barrier_semaphore()
    for bit in range(dp_bits):
        pl.semaphore_signal(
            barrier, inc=1, device_id={"dp": partner(me, bit)}, device_id_type=pl.DeviceIdType.MESH
        )
    own = [
        pltpu.make_async_copy(blocks[array], outs[array].at[me], own_sems.at[array])
        for array in range(count)
    ]
    for copy in own:
        copy.start()
    for copy in own:
        copy.wait()
    pl.semaphore_wait(barrier, dp_bits)
    used = [0]
    pending = {part: [] for part in parts}
    for step in range(dp_bits):
        for array, stream in parts:
            order = orders[stream]
            half = blocks[array].shape[1] // 2
            for copy in pending[array, stream]:
                copy.wait()
            pending[array, stream] = []
            for slot in range(2**step):
                block = me
                for level in range(step):
                    if (slot >> level) & 1:
                        block = block + (1 - 2 * bit_of(me, order[level])) * 2 ** order[level]
                place = outs[array].at[block, :, pl.ds(stream * half, half)]
                copy = pltpu.make_async_remote_copy(
                    src_ref=place,
                    dst_ref=place,
                    send_sem=send_sems.at[used[0]],
                    recv_sem=recv_sems.at[used[0]],
                    device_id={"dp": partner(me, order[step])},
                    device_id_type=pl.DeviceIdType.MESH,
                )
                used[0] += 1
                copy.start()
                pending[array, stream].append(copy)
    for part in parts:
        for copy in pending[part]:
            copy.wait()


def gather_all(blocks, collective):
    dp_size = lax.axis_size("dp")
    dp_bits = dp_size.bit_length() - 1
    count = len(blocks)
    total = count * 2 * (dp_size - 1)

    def body(*refs):
        gather_kernel(count, dp_bits, *refs)

    return pl.pallas_call(
        body,
        in_specs=[pl.BlockSpec(memory_space=pltpu.VMEM)] * count,
        out_specs=[pl.BlockSpec(memory_space=pltpu.VMEM)] * count,
        out_shape=[jax.ShapeDtypeStruct((dp_size,) + block.shape, bf16) for block in blocks],
        scratch_shapes=[
            pltpu.SemaphoreType.DMA((total,)),
            pltpu.SemaphoreType.DMA((total,)),
            pltpu.SemaphoreType.DMA((count,)),
        ],
        compiler_params=pltpu.CompilerParams(
            collective_id=collective, has_side_effects=True, vmem_limit_bytes=32 * 1024 * 1024
        ),
        name="weight_gather",
    )(*blocks)


def shards(inputs, attn_gain, qkv_weight, proj_weight, mlp_gain, in_weight, out_weight, cotangent):
    tokens = inputs.shape[0]
    seq_count = lax.axis_size("seq")
    place = lax.axis_index("seq")
    forward = [(i, i + 1) for i in range(seq_count - 1)]
    backward = [(i + 1, i) for i in range(seq_count - 1)]

    share = attn_gain.shape[0]
    lanes = -(-share // 128) * 128
    gains = jnp.concatenate(
        [jnp.pad(gain[None], ((0, 15), (0, lanes - share))) for gain in (attn_gain, mlp_gain)], 1
    )
    qkv_full, gains_full = gather_all([qkv_weight, gains], 2)
    qkv_full = qkv_full.reshape(D, -1)
    attn_full = gains_full[:, 0, :share].reshape(D).astype(f32)
    mlp_full = gains_full[:, 0, lanes : lanes + share].reshape(D).astype(f32)
    proj_full = gather(proj_weight)
    in_full = gather(in_weight)
    out_full = gather(out_weight)

    before = lax.ppermute(inputs[-WINDOW:], "seq", forward)
    after = lax.ppermute(inputs[:WINDOW], "seq", backward)
    x_wide = jnp.concatenate([before, inputs, after], 0).astype(f32)
    xhat_wide, scale_wide = norm_parts(x_wide)
    n1_wide = (xhat_wide * attn_full).astype(bf16)
    projected = jnp.dot(n1_wide, qkv_full, preferred_element_type=f32)
    positions = (place * tokens - WINDOW + jnp.arange(tokens + 2 * WINDOW, dtype=jnp.int32)).astype(
        f32
    )
    cosine, sine = rotary_tables(positions)
    edges = jnp.stack(
        [jnp.where(place == 0, WINDOW, 0), jnp.where(place == seq_count - 1, SPAN - WINDOW, SPAN)]
    ).astype(jnp.int32)
    mixed, probs, query, key, value = attention(edges, projected, cosine, sine)

    residual = inputs.astype(f32)
    hidden = residual + jnp.dot(mixed, proj_full, preferred_element_type=f32)
    xhat_two, scale_two = norm_parts(hidden)
    n2 = (xhat_two * mlp_full).astype(bf16)
    up = jnp.dot(n2, in_full, preferred_element_type=f32)
    a, g = up[:, :FF], up[:, FF:]
    cdf = 0.5 * (1.0 + lax.erf(a * (0.5**0.5)))
    gelu = a * cdf
    gelu_slope = cdf + a * (jnp.exp(-0.5 * a * a) * (0.5 / jnp.pi) ** 0.5)
    m = (gelu * g).astype(bf16)
    output = (hidden + jnp.dot(m, out_full, preferred_element_type=f32)).astype(bf16)

    out_grad = jnp.einsum("tf,td->fd", m, cotangent, preferred_element_type=f32)
    dm = jnp.einsum("td,fd->tf", cotangent, out_full, preferred_element_type=f32)
    du = jnp.concatenate([dm * g * gelu_slope, dm * gelu], 1).astype(bf16)
    in_grad = jnp.einsum("td,tf->df", n2, du, preferred_element_type=f32)
    dn2 = jnp.einsum("tf,df->td", du, in_full, preferred_element_type=f32)
    dh = cotangent.astype(f32) + norm_back(dn2 * mlp_full, xhat_two, scale_two)
    da = dh.astype(bf16)
    proj_grad = jnp.einsum("te,td->ed", mixed, da, preferred_element_type=f32)
    grad_mixed = jnp.einsum("td,ed->te", da, proj_full, preferred_element_type=f32).astype(bf16)

    dq, dk_wide, dv_wide = attention_back(grad_mixed, query, key, value, probs, cosine, sine)
    own = slice(WINDOW, WINDOW + tokens)
    kv_head = jnp.concatenate([dk_wide[:WINDOW], dv_wide[:WINDOW]], 1)
    kv_tail = jnp.concatenate([dk_wide[-WINDOW:], dv_wide[-WINDOW:]], 1)
    from_after = lax.ppermute(kv_head, "seq", backward)
    from_before = lax.ppermute(kv_tail, "seq", forward)
    qkv_grad = jnp.concatenate(
        [
            dot_first(n1_wide[own], dq).astype(bf16),
            dot_first(n1_wide, dk_wide).astype(bf16),
            dot_first(n1_wide, dv_wide).astype(bf16),
        ],
        1,
    )
    kv = jnp.concatenate([dk_wide[own], dv_wide[own]], 1)
    kv = jnp.concatenate(
        [
            (kv[:WINDOW].astype(f32) + from_before.astype(f32)).astype(bf16),
            kv[WINDOW:-WINDOW],
            (kv[-WINDOW:].astype(f32) + from_after.astype(f32)).astype(bf16),
        ],
        0,
    )
    dproj = jnp.concatenate([dq, kv], 1)
    dn1 = dot_last(dproj, qkv_full)
    xhat_one, scale_one = norm_parts(residual)
    input_grad = (dh + norm_back(dn1 * attn_full, xhat_one, scale_one)).astype(bf16)

    out_total, in_total, proj_total, qkv_total = reduce_all(
        [out_grad, in_grad, proj_grad, qkv_grad], 1
    )
    attn_gain_grad = jnp.sum(qkv_weight.astype(f32) * qkv_total, -1) / attn_gain.astype(f32)
    mlp_gain_grad = jnp.sum(in_weight.astype(f32) * in_total, -1) / mlp_gain.astype(f32)
    return (
        output,
        input_grad,
        attn_gain_grad,
        qkv_total,
        proj_total,
        mlp_gain_grad,
        in_total,
        out_total,
    )


def solution(mesh):
    rows, split = P(("dp", "seq"), None), P("dp", None)
    in_specs = (rows, P("dp"), split, split, P("dp"), split, split, rows)
    out_specs = (rows, rows, P("dp"), split, split, P("dp"), split, split)
    return jax.shard_map(shards, mesh=mesh, in_specs=in_specs, out_specs=out_specs, check_vma=False)
```
